32 devices in a mesh: chan: 8 (over z, x), seg: 4 (over y, core).
Axes of the slice: x: 2, y: 2, z: 4, core: 2. Of those that a mesh axis runs over, the one named last changes fastest.
Arguments:
- spectra: bfloat16 [32, 128, 2, 1024], P(None, 'seg', None, 'chan'), may hold values from -6 to 6
- plan: int32 [4, 8], replicated, may hold values from 0 to 7, as said below
- assignment: int32 [1024], P('chan'), may hold values from 0 to 1023, as said below
Outputs:
- cross_spectra: float32 [4, 32, 2, 1024, 128], P(None, 'seg', None, 'chan')
The draws below stay inside these ranges and needn't reach their ends.
Inputs may be any that keep to these rules, and one draw needn't show every extreme that they name: Each row is a pairing of the blocks: plan[r, plan[r, b]] = b and plan[r, b] != b; no two blocks are paired in two different rounds. `assignment`: entries b * 128 to (b + 1) * 128 - 1 are a permutation of that same range of channels.
All inputs are finite; a program needn't handle non-finite values.
Results may differ from the reference program's by a relative error of at most 0.0003.
Values may be sent and summed in bfloat16 or wider, within the bound.
A program may use at most 128 MiB of HBM per device.

```python
import math
import jax
import jax.numpy as jnp
from jax import lax

CH_BLK = 128
F = 32
ROUNDS = 4
CHANNELS = 1024
WINDOWS = 128
N_CHAN = 8


def draw_plan(key, part):
    group_count = N_CHAN
    odd_count = N_CHAN - 1
    first_key, second_key = jax.random.split(jax.random.fold_in(key, 11))
    round_turns = jax.random.permutation(first_key, odd_count)[:ROUNDS].astype(jnp.int32)
    labels = jax.random.permutation(second_key, group_count).astype(jnp.int32)
    places = jnp.arange(group_count, dtype=jnp.int32)
    mirror = jnp.mod(2 * round_turns[:, None] - places[None, :], odd_count)
    partner_place = jnp.where(places[None, :] == odd_count, round_turns[:, None], jnp.where(mirror == places[None, :], odd_count, mirror))
    sched_table = jnp.zeros((ROUNDS, group_count), jnp.int32).at[:, labels].set(labels[partner_place])
    return sched_table


def draw_assignment(key, part):
    block_keys = jax.random.split(jax.random.fold_in(key, 23), N_CHAN)
    shuffles = jax.vmap(lambda one_key: jax.random.permutation(one_key, CH_BLK))(block_keys)
    offsets = jnp.arange(N_CHAN, dtype=jnp.int32)[:, None] * CH_BLK
    return (shuffles.astype(jnp.int32) + offsets).reshape(N_CHAN * CH_BLK)


def steps_of(key, extent, shards, smallest, high):
    level = 1.0
    for axis_at, shards_of in shards:
        heights = jax.random.uniform(jax.random.fold_in(jax.random.fold_in(key, 6), axis_at), (shards_of,), jnp.float32, smallest / len(shards), high / len(shards))
        level = level * jnp.repeat(jnp.exp(heights), extent[axis_at] // shards_of).reshape((-1,) + (1,) * (len(extent) - 1 - axis_at))
    return level


def scatter_about(rng, shape, scale, limit, cuts=(), kind=jnp.bfloat16):
    drawn = jax.random.normal(rng, shape, jnp.float32) * scale
    if len(cuts) > 0:
        drawn = steps_of(rng, shape, cuts, -0.22, 0.18) * drawn
    return jnp.clip(drawn, min=-limit, max=limit).astype(kind)


def setup_inputs(seed: int = 0) -> dict:
    streams_of = jax.random.split(jax.random.key(seed), 4)
    spectra = scatter_about(streams_of[0], (F, WINDOWS, 2, CHANNELS), 1.0, 6.0, ((1, 4), (3, 8)))
    plan = draw_plan(jax.random.fold_in(streams_of[3], 71), 0)
    assignment = draw_assignment(jax.random.fold_in(streams_of[3], 71), 0)
    return dict(spectra=spectra, plan=plan, assignment=assignment)


def reference(spectra, plan, assignment):
    ordered = jnp.take(spectra, assignment, axis=3)
    scale = 1.0 / math.sqrt(WINDOWS)

    def one_block(pair_index):
        own_block = lax.dynamic_slice_in_dim(ordered, (pair_index[0] * CH_BLK).astype(jnp.int32), CH_BLK, 3).astype(jnp.float32)
        other_block = lax.dynamic_slice_in_dim(ordered, (pair_index[1] * CH_BLK).astype(jnp.int32), CH_BLK, 3).astype(jnp.float32)
        real_part = jnp.einsum('fwc,fwd->fcd', own_block[:, :, 0], other_block[:, :, 0]) + jnp.einsum('fwc,fwd->fcd', own_block[:, :, 1], other_block[:, :, 1])
        imag_part = jnp.einsum('fwc,fwd->fcd', own_block[:, :, 1], other_block[:, :, 0]) - jnp.einsum('fwc,fwd->fcd', own_block[:, :, 0], other_block[:, :, 1])
        return jnp.stack([real_part, imag_part], axis=1) * scale
    rounds_out = []
    for round_index in range(ROUNDS):
        block_ids = jnp.arange(N_CHAN, dtype=jnp.int32)
        blocks = lax.map(one_block, jnp.stack([block_ids, plan[round_index].astype(jnp.int32)], axis=1))
        blocks = jnp.moveaxis(blocks, 0, 2).reshape(F, 2, CHANNELS, CH_BLK)
        rounds_out.append(blocks)
    return jnp.stack(rounds_out)
```

```python
import functools
import math

import jax
import jax.numpy as jnp
from jax import lax
from jax.experimental import pallas as pl
from jax.experimental.pallas import tpu as pltpu
from jax.sharding import PartitionSpec as P

MESH = pl.DeviceIdType.MESH


def ring_place(chan, n_chan):
    z, x = chan // 2, chan % 2
    return z + x * (n_chan - 1 - 2 * z)


def ring_chan(place, n_chan):
    x = place // (n_chan // 2)
    z = place + x * (n_chan - 1 - 2 * place)
    return 2 * z + x


def seg_peer(seg, step, n_seg):
    pair = (seg // 2 + step // 2) % (n_seg // 2)
    return 2 * pair + (seg % 2 + step) % 2


def gather_kernel(n_chan, n_seg, slots_ref, x_ref, out_ref, sorted_ref, own_sem, seg_send, seg_recv, ring_send, ring_recv):
    chan, seg = lax.axis_index("chan"), lax.axis_index("seg")
    place = ring_place(chan, n_chan)
    sides = (
        ring_chan((place + 1) % n_chan, n_chan),
        ring_chan((place + n_chan - 1) % n_chan, n_chan),
    )
    peers = [seg_peer(seg, step, n_seg) for step in range(n_seg)]
    _, bins, rows, width = sorted_ref.shape

    barrier = pltpu.get_barrier_semaphore()
    for side in sides:
        pl.semaphore_signal(barrier, inc=1, device_id=(side, seg), device_id_type=MESH)
    for peer in peers[1:]:
        pl.semaphore_signal(barrier, inc=1, device_id=(chan, peer), device_id_type=MESH)

    column = lax.broadcasted_iota(jnp.int32, (width, width), 0)
    pick = (column == slots_ref[...]).astype(jnp.float32).astype(jnp.bfloat16)

    def sort_part(step):
        part = x_ref[pl.ds(peers[step] * bins, bins)].reshape(bins * rows, width)
        part = jnp.dot(part, pick, preferred_element_type=jnp.float32)
        sorted_ref[step] = part.astype(jnp.bfloat16).reshape(bins, rows, width)

    hops = n_chan // 2

    def ring_copy(way, hop, part):
        held = (n_chan - hop) % n_chan if way else hop
        lands = n_chan - hop - 1 if way else hop + 1
        source = sorted_ref.at[0] if (hop, part) == (0, 0) else out_ref.at[held, part]
        return pltpu.make_async_remote_copy(
            src_ref=source,
            dst_ref=out_ref.at[lands, part],
            send_sem=ring_send.at[way, hop, part],
            recv_sem=ring_recv.at[way, hop, part],
            device_id=(sides[way], seg),
            device_id_type=MESH,
        )

    def goes(way, hop, part):
        return hop < hops - 1 or (part >= n_seg // 2) == bool(way)

    ring = {
        (way, hop, part): ring_copy(way, hop, part)
        for hop in range(hops)
        for part in range(n_seg)
        for way in range(2)
        if goes(way, hop, part)
    }
    swap = {
        step: pltpu.make_async_remote_copy(
            src_ref=sorted_ref.at[step],
            dst_ref=out_ref.at[0, step],
            send_sem=seg_send.at[step],
            recv_sem=seg_recv.at[step],
            device_id=(chan, peers[step]),
            device_id_type=MESH,
        )
        for step in range(1, n_seg)
    }

    sort_part(0)
    pl.semaphore_wait(barrier, 1 + n_seg)
    ring[0, 0, 0].start()
    ring[1, 0, 0].start()
    for step in list(range(2, n_seg)) + [1]:
        sort_part(step)
        swap[step].start()
    own = pltpu.make_async_copy(sorted_ref.at[0], out_ref.at[0, 0], own_sem)
    own.start()

    for hop in range(hops):
        for part in range(n_seg):
            if hop == 0 and part > 0:
                swap[part].wait_recv()
            for way in range(2):
                if (way, hop, part) in ring and (hop, part) != (0, 0):
                    if hop > 0:
                        ring[way, hop - 1, part].wait_recv()
                    ring[way, hop, part].start()
    own.wait()
    for step in range(1, n_seg):
        swap[step].wait_send()
    for (way, hop, part), copy in ring.items():
        if (way, hop + 1, part) not in ring:
            copy.wait_recv()
        copy.wait_send()


def cross_kernel(scale, held_ref, own_ref, other_ref, out_ref, left_ref):
    _, parts, bins, rows, width = own_ref.shape
    depth = parts * rows

    @pl.when(pl.program_id(0) == 0)
    def _():
        row = lax.broadcasted_iota(jnp.int32, (depth, depth), 0)
        col = lax.broadcasted_iota(jnp.int32, (depth, depth), 1)
        up = ((row % 2 == 0) & (col == row + 1)).astype(jnp.float32)
        down = ((row % 2 == 1) & (col == row - 1)).astype(jnp.float32)
        turn = (up - down).astype(jnp.bfloat16)
        for b in range(bins):
            x = own_ref[0, :, b].reshape(depth, width)
            turned = jnp.dot(turn, x, preferred_element_type=jnp.float32)
            left_ref[b, :width] = x.T
            left_ref[b, width:] = turned.astype(jnp.bfloat16).T

    for b in range(bins):
        y = other_ref[0, :, b].reshape(depth, width)
        both = jnp.dot(left_ref[b], y, preferred_element_type=jnp.float32) * scale
        out_ref[0, b] = both.reshape(2, width, width)


def on_device(n_chan, n_seg, spectra, plan, assignment):
    bin_count, win_count, _, width = spectra.shape
    bins, rows = bin_count // n_seg, 2 * win_count
    rounds = plan.shape[0]
    scale = 1.0 / math.sqrt(win_count * n_seg)
    chan = lax.axis_index("chan")
    slots = (assignment - chan * width).reshape(1, width)
    hops = n_chan // 2
    gathered = pl.pallas_call(
        functools.partial(gather_kernel, n_chan, n_seg),
        out_shape=jax.ShapeDtypeStruct((n_chan, n_seg, bins, rows, width), jnp.bfloat16),
        in_specs=[pl.BlockSpec(memory_space=pltpu.VMEM)] * 2,
        out_specs=pl.BlockSpec(memory_space=pl.ANY),
        scratch_shapes=[
            pltpu.VMEM((n_seg, bins, rows, width), jnp.bfloat16),
            pltpu.SemaphoreType.DMA,
            pltpu.SemaphoreType.DMA((n_seg,)),
            pltpu.SemaphoreType.DMA((n_seg,)),
            pltpu.SemaphoreType.DMA((2, hops, n_seg)),
            pltpu.SemaphoreType.DMA((2, hops, n_seg)),
        ],
        compiler_params=pltpu.CompilerParams(collective_id=0, has_side_effects=True),
        name="gather_blocks",
    )(slots, spectra.reshape(bin_count, rows, width))

    partner = lax.dynamic_index_in_dim(plan, chan, 1, keepdims=False)
    held = (ring_place(chan, n_chan) - ring_place(partner, n_chan)) % n_chan
    block = (1, n_seg, bins, rows, width)
    return pl.pallas_call(
        functools.partial(cross_kernel, scale),
        grid_spec=pltpu.PrefetchScalarGridSpec(
            num_scalar_prefetch=1,
            grid=(rounds,),
            in_specs=[
                pl.BlockSpec(block, lambda r, held: (0, 0, 0, 0, 0)),
                pl.BlockSpec(block, lambda r, held: (held[r], 0, 0, 0, 0)),
            ],
            out_specs=pl.BlockSpec((1, bins, 2, width, width), lambda r, held: (r, 0, 0, 0, 0)),
            scratch_shapes=[pltpu.VMEM((bins, 2 * width, n_seg * rows), jnp.bfloat16)],
        ),
        out_shape=jax.ShapeDtypeStruct((rounds, bins, 2, width, width), jnp.float32),
        name="cross_products",
    )(held.astype(jnp.int32), gathered, gathered)


def solution(mesh):
    in_specs = (P(None, "seg", None, "chan"), P(), P("chan"))
    out_specs = P(None, "seg", None, "chan", None)
    return jax.shard_map(
        functools.partial(on_device, mesh.shape["chan"], mesh.shape["seg"]),
        mesh=mesh, in_specs=in_specs, out_specs=out_specs, check_vma=False,
    )
```

```python
import functools
import math

import jax
import jax.numpy as jnp
from jax import lax
from jax.experimental import pallas as pl
from jax.experimental.pallas import tpu as pltpu
from jax.sharding import PartitionSpec as P

MESH = pl.DeviceIdType.MESH


def ring_place(chan, n_chan):
    z, x = chan // 2, chan % 2
    return z + x * (n_chan - 1 - 2 * z)


def ring_chan(place, n_chan):
    x = place // (n_chan // 2)
    z = place + x * (n_chan - 1 - 2 * place)
    return 2 * z + x


def seg_peer(seg, step, n_seg):
    pair = (seg // 2 + step // 2) % (n_seg // 2)
    return 2 * pair + (seg % 2 + step) % 2


def cross_ring_kernel(
    n_chan, n_seg, scale, assign_ref, x_ref, out_ref,
    entry_ref, sorted_ref, block_ref, left_ref, stage_ref,
    entry_sem, stage_sem, seg_send, seg_recv, ring_send, ring_recv,
):
    chan, seg = lax.axis_index("chan"), lax.axis_index("seg")
    place = ring_place(chan, n_chan)
    sides = (
        ring_chan((place + 1) % n_chan, n_chan),
        ring_chan((place + n_chan - 1) % n_chan, n_chan),
    )
    peers = [seg_peer(seg, step, n_seg) for step in range(n_seg)]
    _, bins, rows, width = sorted_ref.shape
    depth = n_seg * rows
    hops = n_chan // 2
    turns = n_seg
    turn_bins = bins // turns

    barrier = pltpu.get_barrier_semaphore()
    for side in sides:
        pl.semaphore_signal(barrier, inc=1, device_id=(side, seg), device_id_type=MESH)
    for peer in peers[1:]:
        pl.semaphore_signal(barrier, inc=1, device_id=(chan, peer), device_id_type=MESH)

    order = [0] + list(range(2, n_seg)) + [1]
    entry = {
        step: pltpu.make_async_copy(
            x_ref.at[pl.ds(peers[step] * bins, bins)], entry_ref.at[step], entry_sem.at[step]
        )
        for step in order
    }
    for step in order:
        entry[step].start()

    column = lax.broadcasted_iota(jnp.int32, (width, width), 0) + chan * width
    pick = (column == assign_ref[...]).astype(jnp.float32).astype(jnp.bfloat16)

    def sort_part(step):
        entry[step].wait()
        part = entry_ref[step].reshape(bins * rows, width)
        part = jnp.dot(part, pick, preferred_element_type=jnp.float32)
        return part.astype(jnp.bfloat16).reshape(bins, rows, width)

    def ring_copy(way, hop, part):
        held = (n_chan - hop) % n_chan if way else hop
        lands = n_chan - hop - 1 if way else hop + 1
        return pltpu.make_async_remote_copy(
            src_ref=block_ref.at[held, part],
            dst_ref=block_ref.at[lands, part],
            send_sem=ring_send.at[way, hop, part],
            recv_sem=ring_recv.at[way, hop, part],
            device_id=(sides[way], seg),
            device_id_type=MESH,
        )

    def goes(way, hop, part):
        return hop < hops - 1 or (part >= n_seg // 2) == bool(way)

    ring = {
        (way, hop, part): ring_copy(way, hop, part)
        for hop in range(hops)
        for part in range(n_seg)
        for way in range(2)
        if goes(way, hop, part)
    }
    swap = {
        step: pltpu.make_async_remote_copy(
            src_ref=sorted_ref.at[step],
            dst_ref=block_ref.at[0, step],
            send_sem=seg_send.at[step],
            recv_sem=seg_recv.at[step],
            device_id=(chan, peers[step]),
            device_id_type=MESH,
        )
        for step in range(1, n_seg)
    }

    def make_left():
        row = lax.broadcasted_iota(jnp.int32, (depth, depth), 0)
        col = lax.broadcasted_iota(jnp.int32, (depth, depth), 1)
        up = ((row % 2 == 0) & (col == row + 1)).astype(jnp.float32)
        down = ((row % 2 == 1) & (col == row - 1)).astype(jnp.float32)
        turn = (up - down).astype(jnp.bfloat16)
        for b in range(bins):
            x = block_ref[0, :, b].reshape(depth, width)
            turned = jnp.dot(turn, x, preferred_element_type=jnp.float32)
            left_ref[b, :width] = x.T
            left_ref[b, width:] = turned.astype(jnp.bfloat16).T

    leaving = {}
    stages = stage_ref.shape[0]

    def product(slot, turn):
        number = 2 * slot - 2 if slot <= hops else 2 * (n_chan - slot) - 1
        stage = number % stages
        if (stage, turn) in leaving:
            leaving[stage, turn].wait()
        for b in range(turn * turn_bins, (turn + 1) * turn_bins):
            y = block_ref[slot, :, b].reshape(depth, width)
            both = jnp.dot(left_ref[b], y, preferred_element_type=jnp.float32) * scale
            stage_ref[stage, b] = both.reshape(2, width, width)
        some = pl.ds(turn * turn_bins, turn_bins)
        leaving[stage, turn] = pltpu.make_async_copy(
            stage_ref.at[stage, some], out_ref.at[slot - 1, some], stage_sem.at[stage, turn]
        )
        leaving[stage, turn].start()

    block_ref[0, 0] = sort_part(0)
    pl.semaphore_wait(barrier, 1 + n_seg)
    ring[0, 0, 0].start()
    ring[1, 0, 0].start()
    for step in order[1:]:
        sorted_ref[step] = sort_part(step)
        swap[step].start()

    for hop in range(hops):
        for part in range(n_seg):
            if hop == 0 and part > 0:
                swap[part].wait_recv()
            for way in range(2):
                if hop > 0 and (way, hop - 1, part) in ring:
                    ring[way, hop - 1, part].wait_recv()
                if (way, hop, part) in ring and (hop, part) != (0, 0):
                    ring[way, hop, part].start()
            if hop > 1:
                product(hop - 1, part)
                product(n_chan - hop + 1, part)
        if hop == 0:
            make_left()
    for turn in range(turns):
        if hops > 1:
            product(hops - 1, turn)
            product(n_chan - hops + 1, turn)
    for part in range(n_seg):
        for way in range(2):
            if (way, hops - 1, part) in ring:
                ring[way, hops - 1, part].wait_recv()
    for turn in range(turns):
        product(hops, turn)
    for step in range(1, n_seg):
        swap[step].wait_send()
    for copy in ring.values():
        copy.wait_send()
    for copy in leaving.values():
        copy.wait()


def choose_kernel(n_chan, plan_ref, product_ref, out_ref, sem):
    chan = lax.axis_index("chan")
    place = ring_place(chan, n_chan)
    copies = []
    for r in range(out_ref.shape[0]):
        away = place + n_chan - ring_place(plan_ref[r, chan], n_chan)
        slot = lax.rem(away, n_chan) - 1
        copies.append(pltpu.make_async_copy(product_ref.at[slot], out_ref.at[r], sem.at[r]))
        copies[-1].start()
    for copy in copies:
        copy.wait()


def on_device(n_chan, n_seg, spectra, plan, assignment):
    bin_count, win_count, _, width = spectra.shape
    bins, rows = bin_count // n_seg, 2 * win_count
    rounds = plan.shape[0]
    scale = 1.0 / math.sqrt(win_count * n_seg)
    hops = n_chan // 2
    part = (n_seg, bins, rows, width)
    spent = 2 * n_chan * n_seg * bins * rows * width
    products = pl.pallas_call(
        functools.partial(cross_ring_kernel, n_chan, n_seg, scale),
        out_shape=jax.ShapeDtypeStruct((n_chan - 1, bins, 2, width, width), jnp.float32),
        in_specs=[pl.BlockSpec(memory_space=pltpu.VMEM), pl.BlockSpec(memory_space=pl.ANY)],
        out_specs=pl.BlockSpec(memory_space=pl.ANY),
        scratch_shapes=[
            pltpu.VMEM(part, jnp.bfloat16),
            pltpu.VMEM(part, jnp.bfloat16),
            pltpu.VMEM((n_chan,) + part, jnp.bfloat16),
            pltpu.VMEM((bins, 2 * width, n_seg * rows), jnp.bfloat16),
            pltpu.VMEM((4, bins, 2, width, width), jnp.float32),
            pltpu.SemaphoreType.DMA((n_seg,)),
            pltpu.SemaphoreType.DMA((4, n_seg)),
            pltpu.SemaphoreType.DMA((n_seg,)),
            pltpu.SemaphoreType.DMA((n_seg,)),
            pltpu.SemaphoreType.DMA((2, hops, n_seg)),
            pltpu.SemaphoreType.DMA((2, hops, n_seg)),
        ],
        compiler_params=pltpu.CompilerParams(
            collective_id=0, has_side_effects=True, vmem_limit_bytes=spent + (14 << 20)
        ),
        name="cross_ring",
    )(assignment.reshape(1, width), spectra.reshape(bin_count, rows, width))

    return pl.pallas_call(
        functools.partial(choose_kernel, n_chan),
        out_shape=jax.ShapeDtypeStruct((rounds, bins, 2, width, width), jnp.float32),
        in_specs=[pl.BlockSpec(memory_space=pltpu.SMEM), pl.BlockSpec(memory_space=pl.ANY)],
        out_specs=pl.BlockSpec(memory_space=pl.ANY),
        scratch_shapes=[pltpu.SemaphoreType.DMA((rounds,))],
        compiler_params=pltpu.CompilerParams(vmem_limit_bytes=4 << 20),
        name="choose_products",
    )(plan, products)


def solution(mesh):
    in_specs = (P(None, "seg", None, "chan"), P(), P("chan"))
    out_specs = P(None, "seg", None, "chan", None)
    return jax.shard_map(
        functools.partial(on_device, mesh.shape["chan"], mesh.shape["seg"]),
        mesh=mesh, in_specs=in_specs, out_specs=out_specs, check_vma=False,
    )
```

```python
import functools
import math

import jax
import jax.numpy as jnp
from jax import lax
from jax.experimental import pallas as pl
from jax.experimental.pallas import tpu as pltpu
from jax.sharding import PartitionSpec as P

MESH = pl.DeviceIdType.MESH


def ring_place(chan, n_chan):
    z, x = chan // 2, chan % 2
    return z + x * (n_chan - 1 - 2 * z)


def ring_chan(place, n_chan):
    x = place // (n_chan // 2)
    z = place + x * (n_chan - 1 - 2 * place)
    return 2 * z + x


def seg_peer(seg, step, n_seg):
    pair = (seg // 2 + step // 2) % (n_seg // 2)
    return 2 * pair + (seg % 2 + step) % 2


def cross_ring_kernel(
    n_chan, n_seg, scale, slots_ref, x_ref, out_ref,
    assign_ref, assign_sem, entry_ref, sorted_ref, block_ref, left_ref, stage_ref,
    entry_sem, stage_sem, seg_send, seg_recv, ring_send, ring_recv,
):
    chan, seg = lax.axis_index("chan"), lax.axis_index("seg")
    place = ring_place(chan, n_chan)
    sides = (
        ring_chan((place + 1) % n_chan, n_chan),
        ring_chan((place + n_chan - 1) % n_chan, n_chan),
    )
    peers = [seg_peer(seg, step, n_seg) for step in range(n_seg)]
    _, bins, rows, width = sorted_ref.shape
    depth = n_seg * rows
    hops = n_chan // 2
    turns = n_seg
    turn_bins = bins // turns

    barrier = pltpu.get_barrier_semaphore()
    for side in sides:
        pl.semaphore_signal(barrier, inc=1, device_id=(side, seg), device_id_type=MESH)
    for peer in peers[1:]:
        pl.semaphore_signal(barrier, inc=1, device_id=(chan, peer), device_id_type=MESH)

    order = [0] + list(range(2, n_seg)) + [1]
    entry = {
        step: pltpu.make_async_copy(
            x_ref.at[pl.ds(peers[step] * bins, bins)], entry_ref.at[step], entry_sem.at[step]
        )
        for step in order
    }
    slots = pltpu.make_async_copy(slots_ref, assign_ref, assign_sem)
    slots.start()
    for step in order:
        entry[step].start()
    slots.wait()

    column = lax.broadcasted_iota(jnp.int32, (width, width), 0) + chan * width
    pick = (column == assign_ref[...]).astype(jnp.float32).astype(jnp.bfloat16)

    def sort_part(step):
        entry[step].wait()
        part = entry_ref[step].reshape(bins * rows, width)
        part = jnp.dot(part, pick, preferred_element_type=jnp.float32)
        return part.astype(jnp.bfloat16).reshape(bins, rows, width)

    def ring_copy(way, hop, part):
        held = (n_chan - hop) % n_chan if way else hop
        lands = n_chan - hop - 1 if way else hop + 1
        return pltpu.make_async_remote_copy(
            src_ref=block_ref.at[held, part],
            dst_ref=block_ref.at[lands, part],
            send_sem=ring_send.at[way, hop, part],
            recv_sem=ring_recv.at[way, hop, part],
            device_id=(sides[way], seg),
            device_id_type=MESH,
        )

    def goes(way, hop, part):
        return hop < hops - 1 or (part >= n_seg // 2) == bool(way)

    ring = {
        (way, hop, part): ring_copy(way, hop, part)
        for hop in range(hops)
        for part in range(n_seg)
        for way in range(2)
        if goes(way, hop, part)
    }
    swap = {
        step: pltpu.make_async_remote_copy(
            src_ref=sorted_ref.at[step],
            dst_ref=block_ref.at[0, step],
            send_sem=seg_send.at[step],
            recv_sem=seg_recv.at[step],
            device_id=(chan, peers[step]),
            device_id_type=MESH,
        )
        for step in range(1, n_seg)
    }

    def make_left():
        row = lax.broadcasted_iota(jnp.int32, (depth, depth), 0)
        col = lax.broadcasted_iota(jnp.int32, (depth, depth), 1)
        up = ((row % 2 == 0) & (col == row + 1)).astype(jnp.float32)
        down = ((row % 2 == 1) & (col == row - 1)).astype(jnp.float32)
        turn = (up - down).astype(jnp.bfloat16)
        for b in range(bins):
            x = block_ref[0, :, b].reshape(depth, width)
            turned = jnp.dot(turn, x, preferred_element_type=jnp.float32)
            left_ref[b, :width] = x.T
            left_ref[b, width:] = turned.astype(jnp.bfloat16).T

    leaving = {}
    stages = stage_ref.shape[0]

    def product(slot, turn):
        number = 2 * slot - 2 if slot <= hops else 2 * (n_chan - slot) - 1
        stage = number % stages
        if (stage, turn) in leaving:
            leaving[stage, turn].wait()
        for b in range(turn * turn_bins, (turn + 1) * turn_bins):
            y = block_ref[slot, :, b].reshape(depth, width)
            both = jnp.dot(left_ref[b], y, preferred_element_type=jnp.float32) * scale
            stage_ref[stage, b] = both.reshape(2, width, width)
        some = pl.ds(turn * turn_bins, turn_bins)
        leaving[stage, turn] = pltpu.make_async_copy(
            stage_ref.at[stage, some], out_ref.at[slot - 1, some], stage_sem.at[stage, turn]
        )
        leaving[stage, turn].start()

    block_ref[0, 0] = sort_part(0)
    pl.semaphore_wait(barrier, 1 + n_seg)
    ring[0, 0, 0].start()
    ring[1, 0, 0].start()
    for step in order[1:]:
        sorted_ref[step] = sort_part(step)
        swap[step].start()

    for hop in range(hops):
        for part in range(n_seg):
            if hop == 0 and part > 0:
                swap[part].wait_recv()
            for way in range(2):
                if hop > 0 and (way, hop - 1, part) in ring:
                    ring[way, hop - 1, part].wait_recv()
                if (way, hop, part) in ring and (hop, part) != (0, 0):
                    ring[way, hop, part].start()
            if hop > 1:
                product(hop - 1, part)
                product(n_chan - hop + 1, part)
        if hop == 0:
            make_left()
    for turn in range(turns):
        if hops > 1:
            product(hops - 1, turn)
            product(n_chan - hops + 1, turn)
    for part in range(n_seg):
        for way in range(2):
            if (way, hops - 1, part) in ring:
                ring[way, hops - 1, part].wait_recv()
    for turn in range(turns):
        product(hops, turn)
    for step in range(1, n_seg):
        swap[step].wait_send()
    for copy in ring.values():
        copy.wait_send()
    for copy in leaving.values():
        copy.wait()


def choose_kernel(n_chan, plan_ref, product_ref, out_ref, sem):
    chan = lax.axis_index("chan")
    place = ring_place(chan, n_chan)
    copies = []
    for r in range(out_ref.shape[0]):
        away = place + n_chan - ring_place(plan_ref[r, chan], n_chan)
        slot = lax.rem(away, n_chan) - 1
        for b in range(out_ref.shape[1]):
            copies.append(pltpu.make_async_copy(product_ref.at[slot, b], out_ref.at[r, b], sem.at[r, b]))
            copies[-1].start()
    for copy in copies:
        copy.wait()


def on_device(n_chan, n_seg, spectra, plan, assignment):
    bin_count, win_count, _, width = spectra.shape
    bins, rows = bin_count // n_seg, 2 * win_count
    rounds = plan.shape[0]
    scale = 1.0 / math.sqrt(win_count * n_seg)
    hops = n_chan // 2
    part = (n_seg, bins, rows, width)
    spent = 2 * n_chan * n_seg * bins * rows * width
    products = pl.pallas_call(
        functools.partial(cross_ring_kernel, n_chan, n_seg, scale),
        out_shape=jax.ShapeDtypeStruct((n_chan - 1, bins, 2, width, width), jnp.float32),
        in_specs=[pl.BlockSpec(memory_space=pltpu.HBM)] * 2,
        out_specs=pl.BlockSpec(memory_space=pl.ANY),
        scratch_shapes=[
            pltpu.VMEM((1, width), jnp.int32),
            pltpu.SemaphoreType.DMA,
            pltpu.VMEM(part, jnp.bfloat16),
            pltpu.VMEM(part, jnp.bfloat16),
            pltpu.VMEM((n_chan,) + part, jnp.bfloat16),
            pltpu.VMEM((bins, 2 * width, n_seg * rows), jnp.bfloat16),
            pltpu.VMEM((4, bins, 2, width, width), jnp.float32),
            pltpu.SemaphoreType.DMA((n_seg,)),
            pltpu.SemaphoreType.DMA((4, n_seg)),
            pltpu.SemaphoreType.DMA((n_seg,)),
            pltpu.SemaphoreType.DMA((n_seg,)),
            pltpu.SemaphoreType.DMA((2, hops, n_seg)),
            pltpu.SemaphoreType.DMA((2, hops, n_seg)),
        ],
        compiler_params=pltpu.CompilerParams(
            collective_id=0, has_side_effects=True, vmem_limit_bytes=spent + (14 << 20)
        ),
        name="cross_ring",
    )(
        pltpu.with_memory_space_constraint(assignment.reshape(1, width), pltpu.HBM),
        pltpu.with_memory_space_constraint(spectra.reshape(bin_count, rows, width), pltpu.HBM),
    )

    return pl.pallas_call(
        functools.partial(choose_kernel, n_chan),
        out_shape=jax.ShapeDtypeStruct((rounds, bins, 2, width, width), jnp.float32),
        in_specs=[pl.BlockSpec(memory_space=pltpu.SMEM), pl.BlockSpec(memory_space=pl.ANY)],
        out_specs=pl.BlockSpec(memory_space=pl.ANY),
        scratch_shapes=[pltpu.SemaphoreType.DMA((rounds, bins))],
        compiler_params=pltpu.CompilerParams(vmem_limit_bytes=4 << 20),
        name="choose_products",
    )(plan, products)


def solution(mesh):
    in_specs = (P(None, "seg", None, "chan"), P(), P("chan"))
    out_specs = P(None, "seg", None, "chan", None)
    return jax.shard_map(
        functools.partial(on_device, mesh.shape["chan"], mesh.shape["seg"]),
        mesh=mesh, in_specs=in_specs, out_specs=out_specs, check_vma=False,
    )
```

```python
import functools
import math

import jax
import jax.numpy as jnp
from jax import lax
from jax.experimental import pallas as pl
from jax.experimental.pallas import tpu as pltpu
from jax.sharding import PartitionSpec as P

MESH = pl.DeviceIdType.MESH


def seg_peer(seg, step, n_seg):
    pair = (seg // 2 + step // 2) % (n_seg // 2)
    return 2 * pair + (seg % 2 + step) % 2


def column_kernel(
    n_chan, n_seg, rounds, slots_ref, plan_ref, x_ref, out_ref, left_out_ref,
    assign_ref, entry_ref, sorted_ref, own_ref, left_ref, keep_ref, give_ref,
    assign_sem, entry_sem, left_sem, keep_sem, own_send, own_recv, mate_send, mate_recv,
    z_send, z_recv, x_send, x_recv, *gathered,
):
    chan, seg = lax.axis_index("chan"), lax.axis_index("seg")
    layers = n_chan // 2
    z, x = chan // 2, chan % 2
    mate = chan + 1 - 2 * x
    peers = [seg_peer(seg, step, n_seg) for step in range(n_seg)]
    _, bins, rows, width = sorted_ref.shape
    depth = n_seg * rows
    half = bins // 2
    subs = 2
    some = half // subs
    chunks = n_seg * subs

    def remote(src, dst, send, recv, to):
        return pltpu.make_async_remote_copy(
            src_ref=src, dst_ref=dst, send_sem=send, recv_sem=recv, device_id=to, device_id_type=MESH
        )

    barrier = pltpu.get_barrier_semaphore()

    def greet(to):
        pl.semaphore_signal(barrier, inc=1, device_id=to, device_id_type=MESH)

    greet((mate, seg))
    for peer in peers[1:]:
        greet((chan, peer))
        greet((mate, peer))

    @pl.when(z > 0)
    def _():
        greet((chan - 2, seg))

    @pl.when(z < layers - 1)
    def _():
        greet((chan + 2, seg))

    order = [0, 1] + list(range(2, n_seg))
    entry = {
        step: pltpu.make_async_copy(
            x_ref.at[pl.ds(peers[step] * bins, bins)], entry_ref.at[step], entry_sem.at[step]
        )
        for step in order
    }
    slots = pltpu.make_async_copy(slots_ref, assign_ref, assign_sem)
    slots.start()
    for step in order:
        entry[step].start()
    slots.wait()

    column = lax.broadcasted_iota(jnp.int32, (width, width), 0) + chan * width
    pick = (column == assign_ref[...]).astype(jnp.float32).astype(jnp.bfloat16)

    def sort_part(step):
        entry[step].wait()
        part = entry_ref[step].reshape(bins * rows, width)
        part = jnp.dot(part, pick, preferred_element_type=jnp.float32)
        return part.astype(jnp.bfloat16).reshape(bins, rows, width)

    def to_own(step):
        return remote(
            sorted_ref.at[step], own_ref.at[step], own_send.at[step], own_recv.at[step],
            (chan, peers[step]),
        )

    def to_mate(step, sub):
        source = own_ref if step == 0 else sorted_ref
        return remote(
            source.at[step, pl.ds((1 - x) * half + sub * some, some)],
            gathered[step * subs + sub].at[chan],
            mate_send.at[step, sub], mate_recv.at[step, sub], (mate, peers[step]),
        )

    def from_mate(step, sub):
        into = gathered[step * subs + sub].at[mate]
        return remote(into, into, mate_send.at[step, sub], mate_recv.at[step, sub], (mate, seg))

    def z_pass(way, chunk, far):
        layer = z + far if way else z - far
        pack = gathered[chunk].at[pl.ds(2 * layer, 2)]
        to = chan - 2 if way else chan + 2
        return remote(pack, pack, z_send.at[way, chunk, far], z_recv.at[way, chunk, far], (to, seg))

    def z_arrival(way, chunk, far):
        layer = z + 1 + far if way else z - 1 - far
        pack = gathered[chunk].at[pl.ds(2 * layer, 2)]
        to = chan + 2 if way else chan - 2
        return remote(pack, pack, z_send.at[way, chunk, far], z_recv.at[way, chunk, far], (to, seg))

    def passes(way, far):
        if way:
            return (z <= layers - 1 - far) & (z >= 1)
        return (z >= far) & (z <= layers - 2)

    def arrives(way, far):
        return z <= layers - 2 - far if way else z >= far + 1

    def place_of(chunk):
        return chunk // subs, chunk % subs

    def x_pass(chunk):
        part, sub = place_of(chunk)
        return remote(
            give_ref.at[chunk], out_ref.at[x, part, sub], x_send.at[chunk], x_recv.at[chunk], (mate, seg)
        )

    def x_arrival(chunk):
        part, sub = place_of(chunk)
        return remote(
            give_ref.at[chunk], out_ref.at[1 - x, part, sub], x_send.at[chunk], x_recv.at[chunk], (mate, seg)
        )

    def keep(chunk):
        part, sub = place_of(chunk)
        return pltpu.make_async_copy(keep_ref.at[chunk], out_ref.at[x, part, sub], keep_sem.at[chunk])

    own_ref[0] = sort_part(0)
    pl.semaphore_wait(barrier, 2 * n_seg - 1 + (z + layers - 1) // layers + (2 * layers - 2 - z) // layers)
    for step in order:
        if step > 0:
            sorted_ref[step] = sort_part(step)
        for sub in range(subs):
            to_mate(step, sub).start()
        if step > 0:
            to_own(step).start()

    def begin(chunk):
        part, sub = place_of(chunk)
        if sub == 0 and part > 0:
            to_own(part).wait_recv()
        gathered[chunk][chan] = own_ref[part, pl.ds(x * half + sub * some, some)]
        from_mate(part, sub).wait_recv()

    def await_layer(way, chunk, far):
        @pl.when(arrives(way, far))
        def _():
            z_arrival(way, chunk, far).wait_recv()

    def send_layer(way, chunk, far):
        @pl.when(passes(way, far))
        def _():
            z_pass(way, chunk, far).start()

    def choose(chunk):
        for r in range(rounds):
            give_ref[chunk, r] = gathered[chunk][plan_ref[r, mate]]
        x_pass(chunk).start()
        for r in range(rounds):
            keep_ref[chunk, r] = gathered[chunk][plan_ref[r, chan]]
        keep(chunk).start()

    def make_left():
        row = lax.broadcasted_iota(jnp.int32, (depth, depth), 0)
        col = lax.broadcasted_iota(jnp.int32, (depth, depth), 1)
        up = ((row % 2 == 0) & (col == row + 1)).astype(jnp.float32)
        down = ((row % 2 == 1) & (col == row - 1)).astype(jnp.float32)
        turn = (up - down).astype(jnp.bfloat16)
        for b in range(bins):
            own = own_ref[:, b].reshape(depth, width)
            turned = jnp.dot(turn, own, preferred_element_type=jnp.float32)
            left_ref[b, :width] = own.T
            left_ref[b, width:] = turned.astype(jnp.bfloat16).T

    left = pltpu.make_async_copy(left_ref, left_out_ref, left_sem)
    for time in range(chunks + layers - 1):
        for far in range(layers - 1):
            chunk = time - far
            if 0 <= chunk < chunks:
                if far == 0:
                    begin(chunk)
                for way in range(2):
                    if far > 0:
                        await_layer(way, chunk, far - 1)
                    send_layer(way, chunk, far)
        if time == chunks - 1:
            make_left()
            left.start()
        last = time - (layers - 1)
        if last >= 0:
            for way in range(2):
                await_layer(way, last, layers - 2)
            choose(last)

    left.wait()
    for step in range(n_seg):
        if step > 0:
            to_own(step).wait_send()
        for sub in range(subs):
            to_mate(step, sub).wait_send()
    for chunk in range(chunks):
        for far in range(layers - 1):
            for way in range(2):
                @pl.when(passes(way, far))
                def _():
                    z_pass(way, chunk, far).wait_send()
    for chunk in range(chunks):
        keep(chunk).wait()
        x_pass(chunk).wait_send()
        x_arrival(chunk).wait_recv()


def cross_kernel(scale, left_ref, other_ref, out_ref):
    _, parts, subs, _, some, rows, width = other_ref.shape
    for b in range(subs * some):
        y = other_ref[0, :, b // some, 0, b % some].reshape(parts * rows, width)
        both = jnp.dot(left_ref[b], y, preferred_element_type=jnp.float32) * scale
        out_ref[0, b] = both.reshape(2, width, width)


def on_device(n_chan, n_seg, spectra, plan, assignment):
    bin_count, win_count, _, width = spectra.shape
    bins, rows = bin_count // n_seg, 2 * win_count
    rounds = plan.shape[0]
    scale = 1.0 / math.sqrt(win_count * n_seg)
    depth = n_seg * rows
    layers = n_chan // 2
    half, subs = bins // 2, 2
    some, chunks = half // subs, n_seg * subs
    part = (n_seg, bins, rows, width)
    chosen = (chunks, rounds, some, rows, width)
    spent = n_chan * n_seg * bins * rows * width
    others, lefts = pl.pallas_call(
        functools.partial(column_kernel, n_chan, n_seg, rounds),
        out_shape=(
            jax.ShapeDtypeStruct((2, n_seg, subs, rounds, some, rows, width), jnp.bfloat16),
            jax.ShapeDtypeStruct((bins, 2 * width, depth), jnp.bfloat16),
        ),
        in_specs=[
            pl.BlockSpec(memory_space=pltpu.HBM),
            pl.BlockSpec(memory_space=pltpu.SMEM),
            pl.BlockSpec(memory_space=pltpu.HBM),
        ],
        out_specs=[pl.BlockSpec(memory_space=pl.ANY)] * 2,
        scratch_shapes=[
            pltpu.VMEM((1, width), jnp.int32),
            pltpu.VMEM(part, jnp.bfloat16),
            pltpu.VMEM(part, jnp.bfloat16),
            pltpu.VMEM(part, jnp.bfloat16),
            pltpu.VMEM((bins, 2 * width, depth), jnp.bfloat16),
            pltpu.VMEM(chosen, jnp.bfloat16),
            pltpu.VMEM(chosen, jnp.bfloat16),
            pltpu.SemaphoreType.DMA,
            pltpu.SemaphoreType.DMA((n_seg,)),
            pltpu.SemaphoreType.DMA,
            pltpu.SemaphoreType.DMA((chunks,)),
            pltpu.SemaphoreType.DMA((n_seg,)),
            pltpu.SemaphoreType.DMA((n_seg,)),
            pltpu.SemaphoreType.DMA((n_seg, subs)),
            pltpu.SemaphoreType.DMA((n_seg, subs)),
            pltpu.SemaphoreType.DMA((2, chunks, layers - 1)),
            pltpu.SemaphoreType.DMA((2, chunks, layers - 1)),
            pltpu.SemaphoreType.DMA((chunks,)),
            pltpu.SemaphoreType.DMA((chunks,)),
        ] + [pltpu.VMEM((n_chan, some, rows, width), jnp.bfloat16)] * chunks,
        compiler_params=pltpu.CompilerParams(
            collective_id=0, has_side_effects=True, vmem_limit_bytes=spent + (16 << 20)
        ),
        name="gather_columns",
    )(
        pltpu.with_memory_space_constraint(assignment.reshape(1, width), pltpu.HBM),
        pltpu.with_memory_space_constraint(plan, pltpu.HBM),
        pltpu.with_memory_space_constraint(spectra.reshape(bin_count, rows, width), pltpu.HBM),
    )

    return pl.pallas_call(
        functools.partial(cross_kernel, scale),
        grid=(2, rounds),
        out_shape=jax.ShapeDtypeStruct((rounds, bins, 2, width, width), jnp.float32),
        in_specs=[
            pl.BlockSpec((half, 2 * width, depth), lambda h, r: (h, 0, 0)),
            pl.BlockSpec((1, n_seg, subs, 1, some, rows, width), lambda h, r: (h, 0, 0, r, 0, 0, 0)),
        ],
        out_specs=pl.BlockSpec((1, half, 2, width, width), lambda h, r: (r, h, 0, 0, 0)),
        compiler_params=pltpu.CompilerParams(vmem_limit_bytes=16 << 20),
        name="cross_products",
    )(lefts, others)


def solution(mesh):
    in_specs = (P(None, "seg", None, "chan"), P(), P("chan"))
    out_specs = P(None, "seg", None, "chan", None)
    return jax.shard_map(
        functools.partial(on_device, mesh.shape["chan"], mesh.shape["seg"]),
        mesh=mesh, in_specs=in_specs, out_specs=out_specs, check_vma=False,
    )
```

```python
import functools
import math

import jax
import jax.numpy as jnp
from jax import lax
from jax.experimental import pallas as pl
from jax.experimental.pallas import tpu as pltpu
from jax.sharding import PartitionSpec as P

MESH = pl.DeviceIdType.MESH


def seg_peer(seg, step, n_seg):
    pair = (seg // 2 + step // 2) % (n_seg // 2)
    return 2 * pair + (seg % 2 + step) % 2


def column_kernel(
    n_chan, n_seg, rounds, slots_ref, plan_ref, x_ref, out_ref, left_out_ref,
    assign_ref, entry_ref, sorted_ref, own_ref, left_ref, keep_ref, give_ref,
    assign_sem, entry_sem, left_sem, keep_sem, own_send, own_recv, mate_send, mate_recv,
    z_send, z_recv, x_send, x_recv, *gathered,
):
    chan, seg = lax.axis_index("chan"), lax.axis_index("seg")
    layers = n_chan // 2
    z, x = chan // 2, chan % 2
    mate = chan + 1 - 2 * x
    peers = [seg_peer(seg, step, n_seg) for step in range(n_seg)]
    _, bins, rows, width = sorted_ref.shape
    depth = n_seg * rows
    half = bins // 2
    subs = 2
    some = half // subs
    chunks = n_seg * subs

    def remote(src, dst, send, recv, to):
        return pltpu.make_async_remote_copy(
            src_ref=src, dst_ref=dst, send_sem=send, recv_sem=recv, device_id=to, device_id_type=MESH
        )

    barrier = pltpu.get_barrier_semaphore()

    def greet(to):
        pl.semaphore_signal(barrier, inc=1, device_id=to, device_id_type=MESH)

    greet((mate, seg))
    for peer in peers[1:]:
        greet((chan, peer))
        greet((mate, peer))

    @pl.when(z > 0)
    def _():
        greet((chan - 2, seg))

    @pl.when(z < layers - 1)
    def _():
        greet((chan + 2, seg))

    order = [0, 1] + list(range(2, n_seg))
    entry = {
        step: pltpu.make_async_copy(
            x_ref.at[pl.ds(peers[step] * bins, bins)], entry_ref.at[step], entry_sem.at[step]
        )
        for step in order
    }
    slots = pltpu.make_async_copy(slots_ref, assign_ref, assign_sem)
    slots.start()
    for step in order:
        entry[step].start()
    slots.wait()

    column = lax.broadcasted_iota(jnp.int32, (width, width), 0) + chan * width
    pick = (column == assign_ref[...]).astype(jnp.float32).astype(jnp.bfloat16)

    def sort_part(step):
        entry[step].wait()
        part = entry_ref[step].reshape(bins * rows, width)
        part = jnp.dot(part, pick, preferred_element_type=jnp.float32)
        return part.astype(jnp.bfloat16).reshape(bins, rows, width)

    def to_own(step):
        return remote(
            sorted_ref.at[step], own_ref.at[step], own_send.at[step], own_recv.at[step],
            (chan, peers[step]),
        )

    def to_mate(step, sub):
        source = own_ref if step == 0 else sorted_ref
        return remote(
            source.at[step, pl.ds((1 - x) * half + sub * some, some)],
            gathered[step * subs + sub].at[chan],
            mate_send.at[step, sub], mate_recv.at[step, sub], (mate, peers[step]),
        )

    def from_mate(step, sub):
        into = gathered[step * subs + sub].at[mate]
        return remote(into, into, mate_send.at[step, sub], mate_recv.at[step, sub], (mate, seg))

    def z_pass(way, chunk, far):
        layer = z + far if way else z - far
        pack = gathered[chunk].at[pl.ds(2 * layer, 2)]
        to = chan - 2 if way else chan + 2
        return remote(pack, pack, z_send.at[way, chunk, far], z_recv.at[way, chunk, far], (to, seg))

    def z_arrival(way, chunk, far):
        layer = z + 1 + far if way else z - 1 - far
        pack = gathered[chunk].at[pl.ds(2 * layer, 2)]
        to = chan + 2 if way else chan - 2
        return remote(pack, pack, z_send.at[way, chunk, far], z_recv.at[way, chunk, far], (to, seg))

    def lag(far):
        return 1 if far > 0 else 2

    def passes(way, far):
        if way:
            return (z <= layers - 1 - far) & (z >= 1)
        return (z >= far) & (z <= layers - 2)

    def arrives(way, far):
        return z <= layers - 2 - far if way else z >= far + 1

    def place_of(chunk):
        return chunk // subs, chunk % subs

    def x_pass(chunk):
        part, sub = place_of(chunk)
        return remote(
            give_ref.at[chunk], out_ref.at[x, part, sub], x_send.at[chunk], x_recv.at[chunk], (mate, seg)
        )

    def x_arrival(chunk):
        part, sub = place_of(chunk)
        return remote(
            give_ref.at[chunk], out_ref.at[1 - x, part, sub], x_send.at[chunk], x_recv.at[chunk], (mate, seg)
        )

    def keep(chunk):
        part, sub = place_of(chunk)
        return pltpu.make_async_copy(keep_ref.at[chunk], out_ref.at[x, part, sub], keep_sem.at[chunk])

    own_ref[0] = sort_part(0)
    pl.semaphore_wait(barrier, 2 * n_seg - 1 + (z + layers - 1) // layers + (2 * layers - 2 - z) // layers)
    for step in order:
        if step > 0:
            sorted_ref[step] = sort_part(step)
        for sub in range(subs):
            to_mate(step, sub).start()
        if step > 0:
            to_own(step).start()

    def begin(chunk):
        part, sub = place_of(chunk)
        if sub == 0 and part > 0:
            to_own(part).wait_recv()
        gathered[chunk][chan] = own_ref[part, pl.ds(x * half + sub * some, some)]
        from_mate(part, sub).wait_recv()

    def await_layer(way, chunk, far):
        @pl.when(arrives(way, far))
        def _():
            z_arrival(way, chunk, far).wait_recv()

    def send_layer(way, chunk, far):
        @pl.when(passes(way, far))
        def _():
            before = chunk - lag(far)
            if before >= 0:
                z_pass(way, before, far).wait_send()
            z_pass(way, chunk, far).start()

    def choose(chunk):
        for r in range(rounds):
            give_ref[chunk, r] = gathered[chunk][plan_ref[r, mate]]
        x_pass(chunk).start()
        for r in range(rounds):
            keep_ref[chunk, r] = gathered[chunk][plan_ref[r, chan]]
        keep(chunk).start()

    def make_left():
        row = lax.broadcasted_iota(jnp.int32, (depth, depth), 0)
        col = lax.broadcasted_iota(jnp.int32, (depth, depth), 1)
        up = ((row % 2 == 0) & (col == row + 1)).astype(jnp.float32)
        down = ((row % 2 == 1) & (col == row - 1)).astype(jnp.float32)
        turn = (up - down).astype(jnp.bfloat16)
        for b in range(bins):
            own = own_ref[:, b].reshape(depth, width)
            turned = jnp.dot(turn, own, preferred_element_type=jnp.float32)
            left_ref[b, :width] = own.T
            left_ref[b, width:] = turned.astype(jnp.bfloat16).T

    left = pltpu.make_async_copy(left_ref, left_out_ref, left_sem)
    for time in range(chunks + layers - 1):
        for far in range(layers - 1):
            chunk = time - far
            if 0 <= chunk < chunks:
                if far == 0:
                    begin(chunk)
                for way in range(2):
                    if far > 0:
                        await_layer(way, chunk, far - 1)
                    send_layer(way, chunk, far)
        if time == chunks - 1:
            make_left()
            left.start()
        last = time - (layers - 1)
        if last >= 0:
            for way in range(2):
                await_layer(way, last, layers - 2)
            choose(last)

    left.wait()
    for step in range(n_seg):
        if step > 0:
            to_own(step).wait_send()
        for sub in range(subs):
            to_mate(step, sub).wait_send()
    for far in range(layers - 1):
        for chunk in range(chunks - lag(far), chunks):
            for way in range(2):
                @pl.when(passes(way, far))
                def _():
                    z_pass(way, chunk, far).wait_send()
    for chunk in range(chunks):
        keep(chunk).wait()
        x_pass(chunk).wait_send()
        x_arrival(chunk).wait_recv()


def cross_kernel(scale, left_ref, other_ref, out_ref):
    _, parts, subs, _, some, rows, width = other_ref.shape
    for b in range(subs * some):
        y = other_ref[0, :, b // some, 0, b % some].reshape(parts * rows, width)
        both = jnp.dot(left_ref[b], y, preferred_element_type=jnp.float32) * scale
        out_ref[0, b] = both.reshape(2, width, width)


def on_device(n_chan, n_seg, spectra, plan, assignment):
    bin_count, win_count, _, width = spectra.shape
    bins, rows = bin_count // n_seg, 2 * win_count
    rounds = plan.shape[0]
    scale = 1.0 / math.sqrt(win_count * n_seg)
    depth = n_seg * rows
    layers = n_chan // 2
    half, subs = bins // 2, 2
    some, chunks = half // subs, n_seg * subs
    part = (n_seg, bins, rows, width)
    chosen = (chunks, rounds, some, rows, width)
    spent = n_chan * n_seg * bins * rows * width
    others, lefts = pl.pallas_call(
        functools.partial(column_kernel, n_chan, n_seg, rounds),
        out_shape=(
            jax.ShapeDtypeStruct((2, n_seg, subs, rounds, some, rows, width), jnp.bfloat16),
            jax.ShapeDtypeStruct((bins, 2 * width, depth), jnp.bfloat16),
        ),
        in_specs=[
            pl.BlockSpec(memory_space=pltpu.HBM),
            pl.BlockSpec(memory_space=pltpu.SMEM),
            pl.BlockSpec(memory_space=pltpu.HBM),
        ],
        out_specs=[pl.BlockSpec(memory_space=pl.ANY)] * 2,
        scratch_shapes=[
            pltpu.VMEM((1, width), jnp.int32),
            pltpu.VMEM(part, jnp.bfloat16),
            pltpu.VMEM(part, jnp.bfloat16),
            pltpu.VMEM(part, jnp.bfloat16),
            pltpu.VMEM((bins, 2 * width, depth), jnp.bfloat16),
            pltpu.VMEM(chosen, jnp.bfloat16),
            pltpu.VMEM(chosen, jnp.bfloat16),
            pltpu.SemaphoreType.DMA,
            pltpu.SemaphoreType.DMA((n_seg,)),
            pltpu.SemaphoreType.DMA,
            pltpu.SemaphoreType.DMA((chunks,)),
            pltpu.SemaphoreType.DMA((n_seg,)),
            pltpu.SemaphoreType.DMA((n_seg,)),
            pltpu.SemaphoreType.DMA((n_seg, subs)),
            pltpu.SemaphoreType.DMA((n_seg, subs)),
            pltpu.SemaphoreType.DMA((2, chunks, layers - 1)),
            pltpu.SemaphoreType.DMA((2, chunks, layers - 1)),
            pltpu.SemaphoreType.DMA((chunks,)),
            pltpu.SemaphoreType.DMA((chunks,)),
        ] + [pltpu.VMEM((n_chan, some, rows, width), jnp.bfloat16)] * chunks,
        compiler_params=pltpu.CompilerParams(
            collective_id=0, has_side_effects=True, vmem_limit_bytes=spent + (16 << 20)
        ),
        name="gather_columns",
    )(
        pltpu.with_memory_space_constraint(assignment.reshape(1, width), pltpu.HBM),
        pltpu.with_memory_space_constraint(plan, pltpu.HBM),
        pltpu.with_memory_space_constraint(spectra.reshape(bin_count, rows, width), pltpu.HBM),
    )

    return pl.pallas_call(
        functools.partial(cross_kernel, scale),
        grid=(2, rounds),
        out_shape=jax.ShapeDtypeStruct((rounds, bins, 2, width, width), jnp.float32),
        in_specs=[
            pl.BlockSpec((half, 2 * width, depth), lambda h, r: (h, 0, 0)),
            pl.BlockSpec((1, n_seg, subs, 1, some, rows, width), lambda h, r: (h, 0, 0, r, 0, 0, 0)),
        ],
        out_specs=pl.BlockSpec((1, half, 2, width, width), lambda h, r: (r, h, 0, 0, 0)),
        compiler_params=pltpu.CompilerParams(vmem_limit_bytes=16 << 20),
        name="cross_products",
    )(lefts, others)


def solution(mesh):
    in_specs = (P(None, "seg", None, "chan"), P(), P("chan"))
    out_specs = P(None, "seg", None, "chan", None)
    return jax.shard_map(
        functools.partial(on_device, mesh.shape["chan"], mesh.shape["seg"]),
        mesh=mesh, in_specs=in_specs, out_specs=out_specs, check_vma=False,
    )
```

```python
import functools
import math

import jax
import jax.numpy as jnp
from jax import lax
from jax.experimental import pallas as pl
from jax.experimental.pallas import tpu as pltpu
from jax.sharding import PartitionSpec as P

MESH = pl.DeviceIdType.MESH


def ring_place(chan, n_chan):
    z, x = chan // 2, chan % 2
    return z + x * (n_chan - 1 - 2 * z)


def ring_chan(place, n_chan):
    x = place // (n_chan // 2)
    z = place + x * (n_chan - 1 - 2 * place)
    return 2 * z + x


def seg_peer(seg, step, n_seg):
    pair = (seg // 2 + step // 2) % (n_seg // 2)
    return 2 * pair + (seg % 2 + step) % 2


def cross_ring_kernel(
    n_chan, n_seg, scale, slots_ref, x_ref, out_ref,
    assign_ref, assign_sem, entry_ref, sorted_ref, block_ref, left_ref, stage_ref,
    entry_sem, stage_sem, seg_send, seg_recv, ring_send, ring_recv,
):
    chan, seg = lax.axis_index("chan"), lax.axis_index("seg")
    place = ring_place(chan, n_chan)
    sides = (
        ring_chan((place + 1) % n_chan, n_chan),
        ring_chan((place + n_chan - 1) % n_chan, n_chan),
    )
    peers = [seg_peer(seg, step, n_seg) for step in range(n_seg)]
    _, bins, rows, width = sorted_ref.shape
    depth = n_seg * rows
    hops = n_chan // 2
    turns = n_seg
    turn_bins = bins // turns

    barrier = pltpu.get_barrier_semaphore()
    for side in sides:
        pl.semaphore_signal(barrier, inc=1, device_id=(side, seg), device_id_type=MESH)
    for peer in peers[1:]:
        pl.semaphore_signal(barrier, inc=1, device_id=(chan, peer), device_id_type=MESH)

    order = [0] + list(range(2, n_seg)) + [1]
    entry = {
        step: pltpu.make_async_copy(
            x_ref.at[pl.ds(peers[step] * bins, bins)], entry_ref.at[step], entry_sem.at[step]
        )
        for step in order
    }
    slots = pltpu.make_async_copy(slots_ref, assign_ref, assign_sem)
    slots.start()
    for step in order:
        entry[step].start()
    slots.wait()

    column = lax.broadcasted_iota(jnp.int32, (width, width), 0) + chan * width
    pick = (column == assign_ref[...]).astype(jnp.float32).astype(jnp.bfloat16)

    def sort_part(step):
        entry[step].wait()
        part = entry_ref[step].reshape(bins * rows, width)
        part = jnp.dot(part, pick, preferred_element_type=jnp.float32)
        return part.astype(jnp.bfloat16).reshape(bins, rows, width)

    def ring_copy(way, hop, part):
        held = (n_chan - hop) % n_chan if way else hop
        lands = n_chan - hop - 1 if way else hop + 1
        return pltpu.make_async_remote_copy(
            src_ref=block_ref.at[held, part],
            dst_ref=block_ref.at[lands, part],
            send_sem=ring_send.at[way, hop, part],
            recv_sem=ring_recv.at[way, hop, part],
            device_id=(sides[way], seg),
            device_id_type=MESH,
        )

    def goes(way, hop, part):
        return hop < hops - 1 or (part >= n_seg // 2) == bool(way)

    ring = {
        (way, hop, part): ring_copy(way, hop, part)
        for hop in range(hops)
        for part in range(n_seg)
        for way in range(2)
        if goes(way, hop, part)
    }
    swap = {
        step: pltpu.make_async_remote_copy(
            src_ref=sorted_ref.at[step],
            dst_ref=block_ref.at[0, step],
            send_sem=seg_send.at[step],
            recv_sem=seg_recv.at[step],
            device_id=(chan, peers[step]),
            device_id_type=MESH,
        )
        for step in range(1, n_seg)
    }

    def make_left():
        row = lax.broadcasted_iota(jnp.int32, (depth, depth), 0)
        col = lax.broadcasted_iota(jnp.int32, (depth, depth), 1)
        up = ((row % 2 == 0) & (col == row + 1)).astype(jnp.float32)
        down = ((row % 2 == 1) & (col == row - 1)).astype(jnp.float32)
        turn = (up - down).astype(jnp.bfloat16)
        for b in range(bins):
            x = block_ref[0, :, b].reshape(depth, width)
            turned = jnp.dot(turn, x, preferred_element_type=jnp.float32)
            left_ref[b, :width] = x.T
            left_ref[b, width:] = turned.astype(jnp.bfloat16).T

    leaving = {}
    stages = stage_ref.shape[0]

    def product(slot, turn):
        number = 2 * slot - 2 if slot <= hops else 2 * (n_chan - slot) - 1
        stage = number % stages
        if (stage, turn) in leaving:
            leaving[stage, turn].wait()
        for b in range(turn * turn_bins, (turn + 1) * turn_bins):
            y = block_ref[slot, :, b].reshape(depth, width)
            both = jnp.dot(left_ref[b], y, preferred_element_type=jnp.float32) * scale
            stage_ref[stage, b] = both.reshape(2, width, width)
        some = pl.ds(turn * turn_bins, turn_bins)
        leaving[stage, turn] = pltpu.make_async_copy(
            stage_ref.at[stage, some], out_ref.at[slot - 1, some], stage_sem.at[stage, turn]
        )
        leaving[stage, turn].start()

    block_ref[0, 0] = sort_part(0)
    pl.semaphore_wait(barrier, 1 + n_seg)
    ring[0, 0, 0].start()
    ring[1, 0, 0].start()
    for step in order[1:]:
        sorted_ref[step] = sort_part(step)
        swap[step].start()

    early, late = range(n_seg // 2), range(n_seg // 2, n_seg)
    visits = [(0, early), (1, early), (0, late), (1, late)]
    visits += [(hop, parts) for hop in range(2, hops) for parts in (early, late)]
    for hop, parts in visits:
        for part in parts:
            if hop == 0 and part > 0:
                swap[part].wait_recv()
            for way in range(2):
                if hop > 0 and (way, hop - 1, part) in ring:
                    ring[way, hop - 1, part].wait_recv()
                if (way, hop, part) in ring and (hop, part) != (0, 0):
                    ring[way, hop, part].start()
            if hop > 1:
                product(hop - 1, part)
                product(n_chan - hop + 1, part)
        if hop == 1 and parts is late:
            make_left()
    for turn in range(turns):
        if hops > 1:
            product(hops - 1, turn)
            product(n_chan - hops + 1, turn)
    for part in range(n_seg):
        for way in range(2):
            if (way, hops - 1, part) in ring:
                ring[way, hops - 1, part].wait_recv()
    for turn in range(turns):
        product(hops, turn)
    for step in range(1, n_seg):
        swap[step].wait_send()
    for copy in ring.values():
        copy.wait_send()
    for copy in leaving.values():
        copy.wait()


def choose_kernel(n_chan, plan_ref, product_ref, out_ref, sem):
    chan = lax.axis_index("chan")
    place = ring_place(chan, n_chan)
    copies = []
    for r in range(out_ref.shape[0]):
        away = place + n_chan - ring_place(plan_ref[r, chan], n_chan)
        slot = lax.rem(away, n_chan) - 1
        copies.append(pltpu.make_async_copy(product_ref.at[slot], out_ref.at[r], sem.at[r]))
        copies[-1].start()
    for copy in copies:
        copy.wait()


def on_device(n_chan, n_seg, spectra, plan, assignment):
    bin_count, win_count, _, width = spectra.shape
    bins, rows = bin_count // n_seg, 2 * win_count
    rounds = plan.shape[0]
    scale = 1.0 / math.sqrt(win_count * n_seg)
    hops = n_chan // 2
    part = (n_seg, bins, rows, width)
    spent = 2 * n_chan * n_seg * bins * rows * width
    products = pl.pallas_call(
        functools.partial(cross_ring_kernel, n_chan, n_seg, scale),
        out_shape=jax.ShapeDtypeStruct((n_chan - 1, bins, 2, width, width), jnp.float32),
        in_specs=[pl.BlockSpec(memory_space=pltpu.HBM)] * 2,
        out_specs=pl.BlockSpec(memory_space=pl.ANY),
        scratch_shapes=[
            pltpu.VMEM((1, width), jnp.int32),
            pltpu.SemaphoreType.DMA,
            pltpu.VMEM(part, jnp.bfloat16),
            pltpu.VMEM(part, jnp.bfloat16),
            pltpu.VMEM((n_chan,) + part, jnp.bfloat16),
            pltpu.VMEM((bins, 2 * width, n_seg * rows), jnp.bfloat16),
            pltpu.VMEM((4, bins, 2, width, width), jnp.float32),
            pltpu.SemaphoreType.DMA((n_seg,)),
            pltpu.SemaphoreType.DMA((4, n_seg)),
            pltpu.SemaphoreType.DMA((n_seg,)),
            pltpu.SemaphoreType.DMA((n_seg,)),
            pltpu.SemaphoreType.DMA((2, hops, n_seg)),
            pltpu.SemaphoreType.DMA((2, hops, n_seg)),
        ],
        compiler_params=pltpu.CompilerParams(
            collective_id=0, has_side_effects=True, vmem_limit_bytes=spent + (14 << 20)
        ),
        name="cross_ring",
    )(
        pltpu.with_memory_space_constraint(assignment.reshape(1, width), pltpu.HBM),
        pltpu.with_memory_space_constraint(spectra.reshape(bin_count, rows, width), pltpu.HBM),
    )

    return pl.pallas_call(
        functools.partial(choose_kernel, n_chan),
        out_shape=jax.ShapeDtypeStruct((rounds, bins, 2, width, width), jnp.float32),
        in_specs=[pl.BlockSpec(memory_space=pltpu.SMEM), pl.BlockSpec(memory_space=pl.ANY)],
        out_specs=pl.BlockSpec(memory_space=pl.ANY),
        scratch_shapes=[pltpu.SemaphoreType.DMA((rounds,))],
        compiler_params=pltpu.CompilerParams(vmem_limit_bytes=4 << 20),
        name="choose_products",
    )(plan, products)


def solution(mesh):
    in_specs = (P(None, "seg", None, "chan"), P(), P("chan"))
    out_specs = P(None, "seg", None, "chan", None)
    return jax.shard_map(
        functools.partial(on_device, mesh.shape["chan"], mesh.shape["seg"]),
        mesh=mesh, in_specs=in_specs, out_specs=out_specs, check_vma=False,
    )
```

```python
import functools
import math

import jax
import jax.numpy as jnp
from jax import lax
from jax.experimental import pallas as pl
from jax.experimental.pallas import tpu as pltpu
from jax.sharding import PartitionSpec as P

MESH = pl.DeviceIdType.MESH


def ring_place(chan, n_chan):
    z, x = chan // 2, chan % 2
    return z + x * (n_chan - 1 - 2 * z)


def ring_chan(place, n_chan):
    x = place // (n_chan // 2)
    z = place + x * (n_chan - 1 - 2 * place)
    return 2 * z + x


def seg_peer(seg, step, n_seg):
    pair = (seg // 2 + step // 2) % (n_seg // 2)
    return 2 * pair + (seg % 2 + step) % 2


def cross_ring_kernel(
    n_chan, n_seg, scale, slots_ref, x_ref, out_ref, left_out_ref, last_ref,
    assign_ref, assign_sem, entry_ref, sorted_ref, block_ref, left_ref, stage_ref,
    entry_sem, stage_sem, left_sem, last_sem, seg_send, seg_recv, ring_send, ring_recv,
):
    chan, seg = lax.axis_index("chan"), lax.axis_index("seg")
    place = ring_place(chan, n_chan)
    sides = (
        ring_chan((place + 1) % n_chan, n_chan),
        ring_chan((place + n_chan - 1) % n_chan, n_chan),
    )
    peers = [seg_peer(seg, step, n_seg) for step in range(n_seg)]
    _, bins, rows, width = sorted_ref.shape
    depth = n_seg * rows
    hops = n_chan // 2
    turns = n_seg
    turn_bins = bins // turns

    barrier = pltpu.get_barrier_semaphore()
    for side in sides:
        pl.semaphore_signal(barrier, inc=1, device_id=(side, seg), device_id_type=MESH)
    for peer in peers[1:]:
        pl.semaphore_signal(barrier, inc=1, device_id=(chan, peer), device_id_type=MESH)

    order = [0] + list(range(2, n_seg)) + [1]
    entry = {
        step: pltpu.make_async_copy(
            x_ref.at[pl.ds(peers[step] * bins, bins)], entry_ref.at[step], entry_sem.at[step]
        )
        for step in order
    }
    slots = pltpu.make_async_copy(slots_ref, assign_ref, assign_sem)
    slots.start()
    for step in order:
        entry[step].start()
    slots.wait()

    column = lax.broadcasted_iota(jnp.int32, (width, width), 0) + chan * width
    pick = (column == assign_ref[...]).astype(jnp.float32).astype(jnp.bfloat16)

    def sort_part(step):
        entry[step].wait()
        part = entry_ref[step].reshape(bins * rows, width)
        part = jnp.dot(part, pick, preferred_element_type=jnp.float32)
        return part.astype(jnp.bfloat16).reshape(bins, rows, width)

    def ring_copy(way, hop, part):
        held = (n_chan - hop) % n_chan if way else hop
        lands = n_chan - hop - 1 if way else hop + 1
        return pltpu.make_async_remote_copy(
            src_ref=block_ref.at[held, part],
            dst_ref=block_ref.at[lands, part],
            send_sem=ring_send.at[way, hop, part],
            recv_sem=ring_recv.at[way, hop, part],
            device_id=(sides[way], seg),
            device_id_type=MESH,
        )

    def goes(way, hop, part):
        return hop < hops - 1 or (part >= n_seg // 2) == bool(way)

    ring = {
        (way, hop, part): ring_copy(way, hop, part)
        for hop in range(hops)
        for part in range(n_seg)
        for way in range(2)
        if goes(way, hop, part)
    }
    swap = {
        step: pltpu.make_async_remote_copy(
            src_ref=sorted_ref.at[step],
            dst_ref=block_ref.at[0, step],
            send_sem=seg_send.at[step],
            recv_sem=seg_recv.at[step],
            device_id=(chan, peers[step]),
            device_id_type=MESH,
        )
        for step in range(1, n_seg)
    }

    def make_left():
        row = lax.broadcasted_iota(jnp.int32, (depth, depth), 0)
        col = lax.broadcasted_iota(jnp.int32, (depth, depth), 1)
        up = ((row % 2 == 0) & (col == row + 1)).astype(jnp.float32)
        down = ((row % 2 == 1) & (col == row - 1)).astype(jnp.float32)
        turn = (up - down).astype(jnp.bfloat16)
        for b in range(bins):
            x = block_ref[0, :, b].reshape(depth, width)
            turned = jnp.dot(turn, x, preferred_element_type=jnp.float32)
            left_ref[b, :width] = x.T
            left_ref[b, width:] = turned.astype(jnp.bfloat16).T

    left = pltpu.make_async_copy(left_ref, left_out_ref, left_sem)
    last = [
        pltpu.make_async_copy(block_ref.at[hops, part], last_ref.at[part], last_sem.at[part])
        for part in range(n_seg)
    ]
    leaving = {}
    stages = stage_ref.shape[0]

    def product(slot, turn):
        number = 2 * slot - 2 if slot <= hops else 2 * (n_chan - slot) - 1
        stage = number % stages
        if (stage, turn) in leaving:
            leaving[stage, turn].wait()
        for b in range(turn * turn_bins, (turn + 1) * turn_bins):
            y = block_ref[slot, :, b].reshape(depth, width)
            both = jnp.dot(left_ref[b], y, preferred_element_type=jnp.float32) * scale
            stage_ref[stage, b] = both.reshape(2, width, width)
        some = pl.ds(turn * turn_bins, turn_bins)
        leaving[stage, turn] = pltpu.make_async_copy(
            stage_ref.at[stage, some], out_ref.at[slot - 1, some], stage_sem.at[stage, turn]
        )
        leaving[stage, turn].start()

    block_ref[0, 0] = sort_part(0)
    pl.semaphore_wait(barrier, 1 + n_seg)
    ring[0, 0, 0].start()
    ring[1, 0, 0].start()
    for step in order[1:]:
        sorted_ref[step] = sort_part(step)
        swap[step].start()

    early, late = range(n_seg // 2), range(n_seg // 2, n_seg)
    visits = [(0, early), (1, early), (0, late), (1, late)]
    visits += [(hop, parts) for hop in range(2, hops) for parts in (early, late)]
    for hop, parts in visits:
        for part in parts:
            if hop == 0 and part > 0:
                swap[part].wait_recv()
            for way in range(2):
                if hop > 0 and (way, hop - 1, part) in ring:
                    ring[way, hop - 1, part].wait_recv()
                if (way, hop, part) in ring and (hop, part) != (0, 0):
                    ring[way, hop, part].start()
            if hop > 1:
                product(hop - 1, part)
                product(n_chan - hop + 1, part)
        if hop == 1 and parts is late:
            make_left()
            left.start()
    for turn in range(turns):
        if hops > 1:
            product(hops - 1, turn)
            product(n_chan - hops + 1, turn)
    for part in range(n_seg):
        for way in range(2):
            if (way, hops - 1, part) in ring:
                ring[way, hops - 1, part].wait_recv()
        last[part].start()
    left.wait()
    for step in range(1, n_seg):
        swap[step].wait_send()
    for copy in ring.values():
        copy.wait_send()
    for copy in list(leaving.values()) + last:
        copy.wait()


def choose_kernel(n_chan, scale, plan_ref, product_ref, left_ref, last_ref, out_ref, made_ref, sem):
    chan = lax.axis_index("chan")
    place = ring_place(chan, n_chan)
    parts, bins, rows, width = last_ref.shape
    hops = n_chan // 2
    slots, copies, mades = [], [], []
    for r in range(out_ref.shape[0]):
        away = place + n_chan - ring_place(plan_ref[r, chan], n_chan)
        slots.append(lax.rem(away, n_chan))
        copies.append(pltpu.make_async_copy(product_ref.at[slots[r] - 1], out_ref.at[r], sem.at[r]))
        mades.append(pltpu.make_async_copy(made_ref, out_ref.at[r], sem.at[r]))
        pl.when(slots[r] != hops)(copies[r].start)
    for b in range(bins):
        y = last_ref[:, b].reshape(parts * rows, width)
        both = jnp.dot(left_ref[b], y, preferred_element_type=jnp.float32) * scale
        made_ref[b] = both.reshape(2, width, width)
    for r in range(out_ref.shape[0]):
        pl.when(slots[r] == hops)(mades[r].start)
    for copy in copies:
        copy.wait()


def on_device(n_chan, n_seg, spectra, plan, assignment):
    bin_count, win_count, _, width = spectra.shape
    bins, rows = bin_count // n_seg, 2 * win_count
    rounds = plan.shape[0]
    scale = 1.0 / math.sqrt(win_count * n_seg)
    hops = n_chan // 2
    part = (n_seg, bins, rows, width)
    spent = 2 * n_chan * n_seg * bins * rows * width
    products, lefts, last = pl.pallas_call(
        functools.partial(cross_ring_kernel, n_chan, n_seg, scale),
        out_shape=(
            jax.ShapeDtypeStruct((n_chan - 1, bins, 2, width, width), jnp.float32),
            jax.ShapeDtypeStruct((bins, 2 * width, n_seg * rows), jnp.bfloat16),
            jax.ShapeDtypeStruct(part, jnp.bfloat16),
        ),
        in_specs=[pl.BlockSpec(memory_space=pltpu.HBM)] * 2,
        out_specs=[pl.BlockSpec(memory_space=pl.ANY)] * 3,
        scratch_shapes=[
            pltpu.VMEM((1, width), jnp.int32),
            pltpu.SemaphoreType.DMA,
            pltpu.VMEM(part, jnp.bfloat16),
            pltpu.VMEM(part, jnp.bfloat16),
            pltpu.VMEM((n_chan,) + part, jnp.bfloat16),
            pltpu.VMEM((bins, 2 * width, n_seg * rows), jnp.bfloat16),
            pltpu.VMEM((4, bins, 2, width, width), jnp.float32),
            pltpu.SemaphoreType.DMA((n_seg,)),
            pltpu.SemaphoreType.DMA((4, n_seg)),
            pltpu.SemaphoreType.DMA,
            pltpu.SemaphoreType.DMA((n_seg,)),
            pltpu.SemaphoreType.DMA((n_seg,)),
            pltpu.SemaphoreType.DMA((n_seg,)),
            pltpu.SemaphoreType.DMA((2, hops, n_seg)),
            pltpu.SemaphoreType.DMA((2, hops, n_seg)),
        ],
        compiler_params=pltpu.CompilerParams(
            collective_id=0, has_side_effects=True, vmem_limit_bytes=spent + (14 << 20)
        ),
        name="cross_ring",
    )(
        pltpu.with_memory_space_constraint(assignment.reshape(1, width), pltpu.HBM),
        pltpu.with_memory_space_constraint(spectra.reshape(bin_count, rows, width), pltpu.HBM),
    )

    return pl.pallas_call(
        functools.partial(choose_kernel, n_chan, scale),
        out_shape=jax.ShapeDtypeStruct((rounds, bins, 2, width, width), jnp.float32),
        in_specs=[
            pl.BlockSpec(memory_space=pltpu.SMEM),
            pl.BlockSpec(memory_space=pl.ANY),
            pl.BlockSpec(memory_space=pltpu.VMEM),
            pl.BlockSpec(memory_space=pltpu.VMEM),
        ],
        out_specs=pl.BlockSpec(memory_space=pl.ANY),
        scratch_shapes=[
            pltpu.VMEM((bins, 2, width, width), jnp.float32),
            pltpu.SemaphoreType.DMA((rounds,)),
        ],
        compiler_params=pltpu.CompilerParams(vmem_limit_bytes=8 << 20),
        name="choose_products",
    )(plan, products, lefts, last)


def solution(mesh):
    in_specs = (P(None, "seg", None, "chan"), P(), P("chan"))
    out_specs = P(None, "seg", None, "chan", None)
    return jax.shard_map(
        functools.partial(on_device, mesh.shape["chan"], mesh.shape["seg"]),
        mesh=mesh, in_specs=in_specs, out_specs=out_specs, check_vma=False,
    )
```

```python
import functools
import math

import jax
import jax.numpy as jnp
from jax import lax
from jax.experimental import pallas as pl
from jax.experimental.pallas import tpu as pltpu
from jax.sharding import PartitionSpec as P

MESH = pl.DeviceIdType.MESH


def ring_place(chan, n_chan):
    z, x = chan // 2, chan % 2
    return z + x * (n_chan - 1 - 2 * z)


def ring_chan(place, n_chan):
    x = place // (n_chan // 2)
    z = place + x * (n_chan - 1 - 2 * place)
    return 2 * z + x


def seg_peer(seg, step, n_seg):
    pair = (seg // 2 + step // 2) % (n_seg // 2)
    return 2 * pair + (seg % 2 + step) % 2


def cross_ring_kernel(
    n_chan, n_seg, scale, slots_ref, x_ref, out_ref,
    assign_ref, assign_sem, entry_ref, sorted_ref, block_ref, left_ref, stage_ref,
    entry_sem, stage_sem, seg_send, seg_recv, ring_send, ring_recv,
):
    chan, seg = lax.axis_index("chan"), lax.axis_index("seg")
    place = ring_place(chan, n_chan)
    sides = (
        ring_chan((place + 1) % n_chan, n_chan),
        ring_chan((place + n_chan - 1) % n_chan, n_chan),
    )
    peers = [seg_peer(seg, step, n_seg) for step in range(n_seg)]
    _, bins, rows, width = sorted_ref.shape
    depth = n_seg * rows
    hops = n_chan // 2
    turns = n_seg
    turn_bins = bins // turns

    barrier = pltpu.get_barrier_semaphore()
    for side in sides:
        pl.semaphore_signal(barrier, inc=1, device_id=(side, seg), device_id_type=MESH)
    for peer in peers[1:]:
        pl.semaphore_signal(barrier, inc=1, device_id=(chan, peer), device_id_type=MESH)

    order = [0] + list(range(2, n_seg)) + [1]
    entry = {
        step: pltpu.make_async_copy(
            x_ref.at[pl.ds(peers[step] * bins, bins)], entry_ref.at[step], entry_sem.at[step]
        )
        for step in order
    }
    slots = pltpu.make_async_copy(slots_ref, assign_ref, assign_sem)
    slots.start()
    for step in order:
        entry[step].start()
    slots.wait()

    column = lax.broadcasted_iota(jnp.int32, (width, width), 0) + chan * width
    pick = (column == assign_ref[...]).astype(jnp.float32).astype(jnp.bfloat16)

    def sort_part(step):
        entry[step].wait()
        part = entry_ref[step].reshape(bins * rows, width)
        part = jnp.dot(part, pick, preferred_element_type=jnp.float32)
        return part.astype(jnp.bfloat16).reshape(bins, rows, width)

    def ring_copy(way, hop, part):
        held = (n_chan - hop) % n_chan if way else hop
        lands = n_chan - hop - 1 if way else hop + 1
        some = pl.ds(part, n_seg // 2 if hop else 1)
        return pltpu.make_async_remote_copy(
            src_ref=block_ref.at[held, some],
            dst_ref=block_ref.at[lands, some],
            send_sem=ring_send.at[way, hop, part],
            recv_sem=ring_recv.at[way, hop, part],
            device_id=(sides[way], seg),
            device_id_type=MESH,
        )

    def goes(way, hop, part):
        if hop and part % (n_seg // 2):
            return False
        return hop < hops - 1 or (part >= n_seg // 2) == bool(way)

    ring = {
        (way, hop, part): ring_copy(way, hop, part)
        for hop in range(hops)
        for part in range(n_seg)
        for way in range(2)
        if goes(way, hop, part)
    }
    swap = {
        step: pltpu.make_async_remote_copy(
            src_ref=sorted_ref.at[step],
            dst_ref=block_ref.at[0, step],
            send_sem=seg_send.at[step],
            recv_sem=seg_recv.at[step],
            device_id=(chan, peers[step]),
            device_id_type=MESH,
        )
        for step in range(1, n_seg)
    }

    def make_left():
        row = lax.broadcasted_iota(jnp.int32, (depth, depth), 0)
        col = lax.broadcasted_iota(jnp.int32, (depth, depth), 1)
        up = ((row % 2 == 0) & (col == row + 1)).astype(jnp.float32)
        down = ((row % 2 == 1) & (col == row - 1)).astype(jnp.float32)
        turn = (up - down).astype(jnp.bfloat16)
        for b in range(bins):
            x = block_ref[0, :, b].reshape(depth, width)
            turned = jnp.dot(turn, x, preferred_element_type=jnp.float32)
            left_ref[b, :width] = x.T
            left_ref[b, width:] = turned.astype(jnp.bfloat16).T

    leaving = {}
    stages = stage_ref.shape[0]

    def product(slot, turn):
        number = 2 * slot - 2 if slot <= hops else 2 * (n_chan - slot) - 1
        stage = number % stages
        if (stage, turn) in leaving:
            leaving[stage, turn].wait()
        for b in range(turn * turn_bins, (turn + 1) * turn_bins):
            y = block_ref[slot, :, b].reshape(depth, width)
            both = jnp.dot(left_ref[b], y, preferred_element_type=jnp.float32) * scale
            stage_ref[stage, b] = both.reshape(2, width, width)
        some = pl.ds(turn * turn_bins, turn_bins)
        leaving[stage, turn] = pltpu.make_async_copy(
            stage_ref.at[stage, some], out_ref.at[slot - 1, some], stage_sem.at[stage, turn]
        )
        leaving[stage, turn].start()

    block_ref[0, 0] = sort_part(0)
    pl.semaphore_wait(barrier, 1 + n_seg)
    ring[0, 0, 0].start()
    ring[1, 0, 0].start()
    for step in order[1:]:
        sorted_ref[step] = sort_part(step)
        swap[step].start()

    early, late = range(n_seg // 2), range(n_seg // 2, n_seg)
    visits = [(0, early), (1, early), (0, late), (1, late)]
    visits += [(hop, parts) for hop in range(2, hops) for parts in (early, late)]
    for hop, parts in visits:
        for part in parts:
            if hop == 0 and part > 0:
                swap[part].wait_recv()
            for way in range(2):
                if hop == 1 and part == parts[0]:
                    for each in parts:
                        ring[way, 0, each].wait_recv()
                if hop > 1 and (way, hop - 1, part) in ring:
                    ring[way, hop - 1, part].wait_recv()
                if (way, hop, part) in ring and (hop, part) != (0, 0):
                    ring[way, hop, part].start()
            if hop > 1:
                product(hop - 1, part)
                product(n_chan - hop + 1, part)
        if hop == 1 and parts is late:
            make_left()
    for turn in range(turns):
        if hops > 1:
            product(hops - 1, turn)
            product(n_chan - hops + 1, turn)
    for part in range(n_seg):
        for way in range(2):
            if (way, hops - 1, part) in ring:
                ring[way, hops - 1, part].wait_recv()
    for turn in range(turns):
        product(hops, turn)
    for step in range(1, n_seg):
        swap[step].wait_send()
    for copy in ring.values():
        copy.wait_send()
    for copy in leaving.values():
        copy.wait()


def choose_kernel(n_chan, plan_ref, product_ref, out_ref, sem):
    chan = lax.axis_index("chan")
    place = ring_place(chan, n_chan)
    copies = []
    for r in range(out_ref.shape[0]):
        away = place + n_chan - ring_place(plan_ref[r, chan], n_chan)
        slot = lax.rem(away, n_chan) - 1
        copies.append(pltpu.make_async_copy(product_ref.at[slot], out_ref.at[r], sem.at[r]))
        copies[-1].start()
    for copy in copies:
        copy.wait()


def on_device(n_chan, n_seg, spectra, plan, assignment):
    bin_count, win_count, _, width = spectra.shape
    bins, rows = bin_count // n_seg, 2 * win_count
    rounds = plan.shape[0]
    scale = 1.0 / math.sqrt(win_count * n_seg)
    hops = n_chan // 2
    part = (n_seg, bins, rows, width)
    spent = 2 * n_chan * n_seg * bins * rows * width
    products = pl.pallas_call(
        functools.partial(cross_ring_kernel, n_chan, n_seg, scale),
        out_shape=jax.ShapeDtypeStruct((n_chan - 1, bins, 2, width, width), jnp.float32),
        in_specs=[pl.BlockSpec(memory_space=pltpu.HBM)] * 2,
        out_specs=pl.BlockSpec(memory_space=pl.ANY),
        scratch_shapes=[
            pltpu.VMEM((1, width), jnp.int32),
            pltpu.SemaphoreType.DMA,
            pltpu.VMEM(part, jnp.bfloat16),
            pltpu.VMEM(part, jnp.bfloat16),
            pltpu.VMEM((n_chan,) + part, jnp.bfloat16),
            pltpu.VMEM((bins, 2 * width, n_seg * rows), jnp.bfloat16),
            pltpu.VMEM((4, bins, 2, width, width), jnp.float32),
            pltpu.SemaphoreType.DMA((n_seg,)),
            pltpu.SemaphoreType.DMA((4, n_seg)),
            pltpu.SemaphoreType.DMA((n_seg,)),
            pltpu.SemaphoreType.DMA((n_seg,)),
            pltpu.SemaphoreType.DMA((2, hops, n_seg)),
            pltpu.SemaphoreType.DMA((2, hops, n_seg)),
        ],
        compiler_params=pltpu.CompilerParams(
            collective_id=0, has_side_effects=True, vmem_limit_bytes=spent + (14 << 20)
        ),
        name="cross_ring",
    )(
        pltpu.with_memory_space_constraint(assignment.reshape(1, width), pltpu.HBM),
        pltpu.with_memory_space_constraint(spectra.reshape(bin_count, rows, width), pltpu.HBM),
    )

    return pl.pallas_call(
        functools.partial(choose_kernel, n_chan),
        out_shape=jax.ShapeDtypeStruct((rounds, bins, 2, width, width), jnp.float32),
        in_specs=[pl.BlockSpec(memory_space=pltpu.SMEM), pl.BlockSpec(memory_space=pl.ANY)],
        out_specs=pl.BlockSpec(memory_space=pl.ANY),
        scratch_shapes=[pltpu.SemaphoreType.DMA((rounds,))],
        compiler_params=pltpu.CompilerParams(vmem_limit_bytes=4 << 20),
        name="choose_products",
    )(plan, products)


def solution(mesh):
    in_specs = (P(None, "seg", None, "chan"), P(), P("chan"))
    out_specs = P(None, "seg", None, "chan", None)
    return jax.shard_map(
        functools.partial(on_device, mesh.shape["chan"], mesh.shape["seg"]),
        mesh=mesh, in_specs=in_specs, out_specs=out_specs, check_vma=False,
    )
```
